256 devices in a mesh: dp: 32 (over y, x, core), tensor: 8 (over z).
Axes of the slice: x: 4, y: 4, z: 8, core: 2. Of those that a mesh axis runs over, the one named last changes fastest.
Arguments:
- tokens: bfloat16 [16384, 8192], P(('dp', 'tensor')), may hold values from -6 to 6
- gate_grads: bfloat16 [16384, 28672], P('dp', 'tensor'), may hold values from -6 to 6
- up_grads: bfloat16 [16384, 28672], P('dp', 'tensor'), may hold values from -6 to 6
- input_proj: bfloat16 [8192, 128], replicated, may hold values from -0.0625 to 0.0625
- output_proj: bfloat16 [28672, 128], P('tensor'), may hold values from -0.03125 to 0.03125
- segment_ids: int32 [16384], P('dp'), may hold values from 0 to 3, as said below
- doc_lengths: int32 [128], P('dp'), may hold values from 1 to 256, as said below
- input_inverse: float32 [2, 64, 64], replicated, as said below
- output_inverse: float32 [2, 64, 64], replicated, as said below
- queries: float32 [4096, 8192], P('tensor', 'dp'), may hold values from -0.0625 to 0.0625
Outputs:
- scores: float32 [128, 4096], P('dp', 'tensor')
The draws below stay inside these ranges and needn't reach their ends.
Inputs may be any that keep to these rules, and one draw needn't show every extreme that they name: `doc_lengths`: within each aligned group of 4 entries (the documents of one index of dp) the lengths sum to 512, and one of them is exactly 256. `segment_ids`: within each aligned group of 512 tokens the ids never fall, and id e appears exactly as often as the e-th length of the group's documents. `input_inverse`: each of the two matrices is symmetric. `output_inverse`: each of the two matrices is symmetric.
All inputs are finite; a program needn't handle non-finite values.
Results may differ from the reference program's by a relative error of at most 0.0003.
Values sent between devices are 32-bit elements; how exact they have to be, the bound alone decides.
A program may use at most 128 MiB of HBM per device.

```python
import math
import jax
import jax.numpy as jnp
from jax import lax

D = 8192
FF = 28672
R = 64
TOK_DEV = 512
DOC_DEV = 4
NQ = 4096
LEN_MAX = 256
TOKENS = 16384
DOCS = 128
FEAT = 8192


def group_lengths(key):
    key = jax.random.fold_in(key, 11)
    groups = DOCS // DOC_DEV
    spare = TOK_DEV - LEN_MAX - (DOC_DEV - 1)
    cuts = jax.random.randint(key, (groups, DOC_DEV - 2), 0, spare + 1)
    cuts = jnp.sort(cuts, axis=1)
    edges = jnp.concatenate([jnp.zeros((groups, 1), jnp.int32), cuts.astype(jnp.int32), jnp.full((groups, 1), spare, jnp.int32)], axis=1)
    others = 1 + edges[:, 1:] - edges[:, :-1]
    longest = jnp.full((groups, 1), LEN_MAX, jnp.int32)
    joined = jnp.concatenate([longest, others], axis=1)
    shifts = jax.random.randint(jax.random.fold_in(key, 1), (groups,), 0, DOC_DEV)
    return jax.vmap(jnp.roll)(joined, shifts).astype(jnp.int32)


def draw_doc_lengths(key, part):
    return group_lengths(key).reshape(DOCS)


def draw_segment_ids(key, part):
    lengths = group_lengths(key)
    ends = jnp.cumsum(lengths, axis=1)
    places = jnp.arange(TOK_DEV, dtype=jnp.int32)
    below = (ends[:, None, :] <= places[None, :, None]).astype(jnp.int32)
    return jnp.sum(below, axis=2).astype(jnp.int32).reshape(TOKENS)


def symmetric_matrix(scale_key, noise):
    scales = jnp.exp(jax.random.uniform(scale_key, (2, R), minval=-0.7, maxval=0.7))
    off = (noise + jnp.swapaxes(noise, 1, 2)) * (0.5 / math.sqrt(R))
    ident = jnp.eye(R, dtype=jnp.float32)
    return (off * (1.0 - ident)[None] + scales[:, :, None] * ident[None]).astype(jnp.float32)


def draw_input_inverse(key, part):
    key = jax.random.fold_in(key, 3)
    scale_key, noise_key = jax.random.split(key)
    noise = jax.random.normal(noise_key, (2, R, R))
    return symmetric_matrix(scale_key, noise)


def draw_output_inverse(key, part):
    key = jax.random.fold_in(key, 5)
    scale_key, noise_key = jax.random.split(key)
    noise = jax.random.normal(noise_key, (2, R, R))
    return symmetric_matrix(scale_key, noise)


def level_of(rng, shape, shards, least, top_value):
    def one(position, parts):
        steps = jax.random.uniform(jax.random.fold_in(jax.random.fold_in(rng, 6), position), (parts,), jnp.float32, least / len(shards), top_value / len(shards))
        return jnp.repeat(jnp.exp(steps), shape[position] // parts).reshape((-1,) + (1,) * (len(shape) - position - 1))

    gain = one(*shards[0])
    for cut in shards[1:]:
        gain = gain * one(*cut)
    return gain


def scatter_about(own_key, shape, scale, most, pieces=(), kind=jnp.bfloat16):
    loudness = level_of(own_key, shape, pieces, -0.22, 0.18) if pieces else 1.0
    values = jax.random.normal(own_key, shape, jnp.float32) * scale * loudness
    return jnp.minimum(jnp.maximum(values, -most), most).astype(kind)


def setup_inputs(seed: int = 0) -> dict:
    splits = jax.random.split(jax.random.key(seed), 11)
    tokens = scatter_about(splits[0], (TOKENS, D), 1.0, 6.0, ((0, 256),))
    gate_grads = scatter_about(splits[1], (TOKENS, FF), 1.0, 6.0, ((0, 32), (1, 8)))
    up_grads = scatter_about(splits[2], (TOKENS, FF), 1.0, 6.0, ((0, 32), (1, 8)))
    input_proj = scatter_about(splits[3], (D, 2 * R), D ** -0.5, 0.0625)
    output_proj = scatter_about(splits[4], (FF, 2 * R), FF ** -0.5, 0.03125, ((0, 8),))
    segment_ids = draw_segment_ids(jax.random.fold_in(splits[10], 71), 0)
    doc_lengths = draw_doc_lengths(jax.random.fold_in(splits[10], 71), 0)
    input_inverse = draw_input_inverse(jax.random.fold_in(splits[10], 71), 0)
    output_inverse = draw_output_inverse(jax.random.fold_in(splits[10], 71), 0)
    queries = scatter_about(splits[9], (NQ, FEAT), FEAT ** -0.5, 0.0625, ((0, 8), (1, 32)), jnp.float32)
    return {"tokens": tokens, "gate_grads": gate_grads, "up_grads": up_grads, "input_proj": input_proj, "output_proj": output_proj, "segment_ids": segment_ids, "doc_lengths": doc_lengths, "input_inverse": input_inverse, "output_inverse": output_inverse, "queries": queries}


def outer_sums(left_codes, right_codes, segment_rows, doc_lengths):
    count = doc_lengths.shape[0]
    rows = left_codes.shape[0]
    rank = right_codes.shape[1] // 2
    labels = jnp.arange(count, dtype=jnp.int32)
    member = (segment_rows[:, None] == labels[None, :]).astype(jnp.float32)
    weights = member / doc_lengths.astype(jnp.float32)[None, :]
    spread = weights[:, :, None, None] * left_codes.reshape(rows, 1, 2, rank)
    sums = jnp.einsum("temi,tmj->emij", spread, right_codes.reshape(rows, 2, rank), precision=lax.Precision.HIGHEST)
    return sums.reshape(count, 2 * rank * rank)


def condition(examples, input_inverse, output_inverse):
    count = examples.shape[0]
    rank = input_inverse.shape[1]
    blocks = examples.reshape(count, 2, rank, rank)
    left = jnp.einsum("mik,emkj->emij", input_inverse, blocks, precision=lax.Precision.HIGHEST)
    both = jnp.einsum("emik,mkj->emij", left, output_inverse, precision=lax.Precision.HIGHEST)
    return both.reshape(count, 2 * rank * rank)


def reference(tokens, gate_grads, up_grads, input_proj, output_proj, segment_ids, doc_lengths, input_inverse, output_inverse, queries):
    rank = input_inverse.shape[1]
    codes = jnp.dot(tokens, input_proj, preferred_element_type=jnp.float32)
    grad_codes = jnp.concatenate([
        jnp.dot(gate_grads, output_proj[:, :rank], preferred_element_type=jnp.float32),
        jnp.dot(up_grads, output_proj[:, rank:], preferred_element_type=jnp.float32)], axis=1)
    groups = DOCS // DOC_DEV
    per_group = lax.map(
        lambda items: outer_sums(items[0], items[1], items[2], items[3]),
        (codes.reshape(groups, TOK_DEV, 2 * rank),
         grad_codes.reshape(groups, TOK_DEV, 2 * rank),
         segment_ids.reshape(groups, TOK_DEV),
         doc_lengths.reshape(groups, DOC_DEV)))
    examples = per_group.reshape(DOCS, 2 * rank * rank)
    conditioned = condition(examples, input_inverse, output_inverse)
    return jnp.dot(conditioned, queries.T, precision=lax.Precision.HIGHEST)
```

```python
import jax
import jax.numpy as jnp
from jax import lax
from jax.experimental import pallas as pl
from jax.experimental.pallas import tpu as pltpu
from jax.sharding import PartitionSpec as P

F32, BF16 = jnp.float32, jnp.bfloat16
FAR_FIRST = (4, 3, 5, 2, 6, 1, 7)
PEERS = ((2, 1), (2, 0), (1, 1), (3, 1), (1, 0), (3, 0), (0, 1))
CHUNKS = 2
NN = (((1,), (0,)), ((), ()))
NT = (((1,), (1,)), ((), ()))


def mm(a, b, dims):
    return lax.dot_general(a, b, dims, preferred_element_type=F32)


def exact(a, b, dims):
    return lax.dot_general(a, b, dims, precision=lax.Precision.HIGHEST, preferred_element_type=F32)


def split(a):
    hi = a.astype(BF16)
    return hi, (a - hi.astype(F32)).astype(BF16)


def mm3(a, b, dims):
    (ah, al), (bh, bl) = a, b
    return mm(ah, bh, dims) + (mm(ah, bl, dims) + mm(al, bh, dims))


def iota(shape, axis):
    return lax.broadcasted_iota(jnp.int32, shape, axis)


def kernel(
    tokens_hbm, gate_hbm, up_hbm, iproj_hbm, oproj_hbm, seg_hbm, len_hbm, ainv_hbm, binv_hbm, query_hbm,
    out_ref,
    tokens, gate, up, iproj, oproj, seg, lens, ainv, binv, query,
    csend, cbuf, gsend, gbuf, qbuf, qhi, qlo, esend, ebuf, rsum, psend, pbuf,
    load_sem, c_sem, g_send, g_recv, q_send, q_recv, e_sem, p_sem, ready,
):
    d, z = lax.axis_index("dp"), lax.axis_index("tensor")
    y, x, c = d // 8, lax.rem(d // 2, 4), lax.rem(d, 2)
    m, jz = z // 4, lax.rem(z, 4)

    def dp(y_to, x_to, c_to):
        return lax.rem(y_to, 4) * 8 + lax.rem(x_to, 4) * 2 + lax.rem(c_to, 2)

    def ring(k):
        return lax.rem(z + k, 8)

    def send(src, dst, s_sem, r_sem, to):
        copy = pltpu.make_async_remote_copy(
            src_ref=src, dst_ref=dst, send_sem=s_sem, recv_sem=r_sem, device_id=to, device_id_type=pl.DeviceIdType.MESH
        )
        copy.start()

    def took(ref, sem):
        pltpu.make_async_copy(ref, ref, sem).wait()

    left, right = (dp(y, x + 3, c), z), (dp(y, x + 1, c), z)
    peers = [(dp(y + ky, x, c + kc), z) for ky, kc in PEERS]

    tc = gate.shape[0] // CHUNKS
    rows = [pl.ds(n * tc, tc) for n in range(CHUNKS)]
    pairs = [(tokens_hbm, tokens), (iproj_hbm, iproj), (ainv_hbm, ainv), (query_hbm, query), (binv_hbm, binv),
             (oproj_hbm, oproj), (seg_hbm, seg), (len_hbm, lens)]
    for n in range(CHUNKS):
        pairs += [(gate_hbm.at[rows[n]], gate.at[rows[n]]), (up_hbm.at[rows[n]], up.at[rows[n]])]
    loads = [pltpu.make_async_copy(src, dst, load_sem.at[i]) for i, (src, dst) in enumerate(pairs)]
    for load in loads:
        load.start()

    barrier = pltpu.get_barrier_semaphore()
    greet = [(d, ring(k)) for k in FAR_FIRST] + peers + [left, right]
    for to in greet:
        pl.semaphore_signal(barrier, inc=1, device_id=to, device_id_type=pl.DeviceIdType.MESH)

    loads[0].wait()
    loads[1].wait()
    codes = mm(tokens[...], iproj[...], NN)
    loads[2].wait()
    r, i = iota((64, 64), 0), iota((64, 64), 1)
    source = (((r >> 2) & 1) << 5) + ((r & 1) << 4) + (((r >> 5) & 1) << 3) + (((r >> 1) & 1) << 2) + ((r >> 3) & 3)
    order = (source == i).astype(F32)
    halves = [(iota((64, 128), 1) == iota((64, 128), 0) + 64 * n).astype(F32) for n in range(2)]
    left_inverse = jnp.concatenate(
        [exact(exact(order, ainv[n], NN), halves[n], NN) for n in range(2)], axis=0
    )
    both = mm3(split(left_inverse), split(jnp.concatenate([codes, codes], axis=0)), NT)
    low = iota((32, 128), 1) < 64
    for n in range(2):
        csend[n] = jnp.where(low, both[64 * n : 64 * n + 32], both[64 * n + 32 : 64 * n + 64])

    loads[3].wait()
    r, i = iota((256, 256), 0), iota((256, 256), 1)
    shuffle = ((((r >> 4) & 3) << 6) + ((r >> 6) << 4) + (r & 15) == i).astype(BF16)
    q_hi, q_lo = split(query[...])
    qbuf[x] = mm(shuffle, q_hi, NT) + mm(shuffle, q_lo, NT)

    loads[4].wait()
    right_inverse = split(jnp.concatenate([exact(binv[n], halves[n], NN) for n in range(2)], axis=0))

    pl.semaphore_wait(barrier, len(greet))

    for k in FAR_FIRST:
        send(csend.at[ring(k) // 4], cbuf.at[z], c_sem.at[0], c_sem.at[1], (d, ring(k)))
    for to in peers:
        pl.semaphore_signal(ready, inc=1, device_id=to, device_id_type=pl.DeviceIdType.MESH)
    first, second = pl.ds(0, 128), pl.ds(128, 128)
    send(qbuf.at[x, first], qbuf.at[x, first], q_send.at[0], q_recv.at[0], left)
    send(qbuf.at[x, second], qbuf.at[x, second], q_send.at[1], q_recv.at[1], right)
    send(qbuf.at[x, second], qbuf.at[x, second], q_send.at[2], q_recv.at[2], left)
    send(qbuf.at[x, first], qbuf.at[x, first], q_send.at[3], q_recv.at[3], right)
    cbuf[z] = csend[m]

    loads[5].wait()
    low = iota((tc, 128), 1) < 64
    for n in range(CHUNKS):
        loads[8 + 2 * n].wait()
        part = mm(gate[rows[n]], oproj[...], NN)
        loads[9 + 2 * n].wait()
        part = jnp.where(low, part, mm(up[rows[n]], oproj[...], NN))
        gsend[n] = mm3(right_inverse, split(part), NT).reshape(8, 16, tc)
        for k in FAR_FIRST:
            send(gsend.at[n, ring(k)], gbuf.at[n, k - 1], g_send.at[n], g_recv.at[n], (d, ring(k)))

    loads[6].wait()
    loads[7].wait()
    weights = [
        jnp.where(seg[...] == g, 1.0 / jnp.broadcast_to(lens[:, g : g + 1], seg.shape).astype(F32), 0.0) for g in range(4)
    ]

    took(cbuf.at[pl.ds(0, 7)], c_sem.at[1])
    low = iota((32, 128), 1) < 64
    upper, lower = [], []
    for n in range(4):
        even, odd = cbuf[2 * n], cbuf[2 * n + 1]
        upper.append(jnp.where(low, even, pltpu.roll(odd, 64, 1)))
        lower.append(jnp.where(low, pltpu.roll(even, 64, 1), odd))
    codes_t = split(jnp.concatenate([jnp.concatenate(upper, axis=1), jnp.concatenate(lower, axis=1)], axis=0))

    took(qbuf.at[0, first], q_recv.at[0])
    after = lax.rem(x + 1, 4)
    send(qbuf.at[after, first], qbuf.at[after, first], q_send.at[4], q_recv.at[4], left)
    took(qbuf.at[0, first], q_recv.at[1])
    before = lax.rem(x + 3, 4)
    send(qbuf.at[before, second], qbuf.at[before, second], q_send.at[5], q_recv.at[5], right)

    sums = []
    for n in range(CHUNKS):
        took(gbuf.at[n], g_recv.at[n])
        total = gsend[n, z]
        for k in range(7):
            total = total + gbuf[n, k]
        sums.append(total)
    columns = jnp.concatenate(sums, axis=1)
    spread = jnp.concatenate([columns * w for w in weights] * 2, axis=0)
    outer = mm3(codes_t, split(spread), NT)
    turned = [outer] + [pltpu.roll(outer, 16 * k, 1) for k in (1, 2, 3)]
    place = iota((8, 128), 1) >> 4
    for g in range(4):
        piece = turned[(0 - g) % 4][0:8]
        for k in range(1, 8):
            piece = jnp.where(place == k, turned[(k - g) % 4][8 * k : 8 * k + 8], piece)
        esend[pl.ds(g, 8, stride=4), :] = piece

    pl.semaphore_wait(ready, len(peers))
    mine = [[(y == 2 * m + ky) & (c == kc) for kc in range(2)] for ky in range(2)]
    for k in FAR_FIRST + (0,):
        for ky in range(2):
            for kc in range(2):
                y_to, src = 2 * m + ky, esend.at[pl.ds(8 * (2 * ky + kc), 8)]
                slot = (lax.rem(y - y_to + 4, 4) * 2 + lax.rem(c + kc, 2)) * 4 + jz
                dst = ebuf.at[slot]
                to = (dp(y_to, x, kc), ring(k))
                if k:
                    send(src, dst, e_sem.at[0], e_sem.at[1], to)
                else:

                    @pl.when(jnp.logical_not(mine[ky][kc]))
                    def _(src=src, dst=dst, to=to):
                        send(src, dst, e_sem.at[0], e_sem.at[1], to)

                    @pl.when(mine[ky][kc])
                    def _(src=src, dst=dst):
                        pltpu.make_async_copy(src, dst, e_sem.at[1]).start()

    def prepare(block, jzs):
        for n in jzs:
            hi, lo = split(qbuf[block, pl.ds(64 * n, 64)])
            at = pl.ds(pl.multiple_of(lax.rem(block, 2) * 64, 64), 64)
            qhi[block // 2, n, at] = hi
            qlo[block // 2, n, at] = lo

    prepare(x, range(4))
    prepare(after, range(2))
    prepare(before, range(2, 4))
    took(qbuf.at[0, first], q_recv.at[2])
    prepare(after, range(2, 4))
    took(qbuf.at[0, first], q_recv.at[3])
    prepare(before, range(2))
    beyond = lax.rem(x + 2, 4)
    took(qbuf.at[0, first], q_recv.at[4])
    prepare(beyond, range(2))
    took(qbuf.at[0, first], q_recv.at[5])
    prepare(beyond, range(2, 4))

    took(ebuf, e_sem.at[1])
    pieces = ebuf[...].reshape(8, 4, 8, 128)
    e_hi, e_lo = split(jnp.concatenate([pieces[:, n].reshape(64, 128) for n in range(4)], axis=1))
    e_both = jnp.concatenate([e_hi, e_lo], axis=0)
    part = []
    for n in range(2):
        main = mm(e_both, qhi[n].reshape(512, 512), NN)
        part.append(main[:64] + main[64:] + mm(e_hi, qlo[n].reshape(512, 512), NN))
    rsum[...] = part[1]
    for n in range(8):
        psend[n] = part[0][8 * n : 8 * n + 4] + rsum[8 * n + 4 : 8 * n + 8]
    for (ky, kc), to in zip(PEERS, peers, strict=True):
        n = 2 * ky + kc
        send(psend.at[n], pbuf.at[n - 1], p_sem.at[0], p_sem.at[1], to)
    took(pbuf, p_sem.at[1])
    total = psend[0]
    for n in range(7):
        total = total + pbuf[n]
    out_ref[...] = total

    took(cbuf.at[pl.ds(0, 7)], c_sem.at[0])
    for n in range(CHUNKS):
        took(gbuf.at[n], g_send.at[n])
    for n in range(6):
        took(qbuf.at[0, first], q_send.at[n])
    took(ebuf.at[pl.ds(0, 31)], e_sem.at[0])

    @pl.when(m != y // 2)
    def _():
        took(ebuf.at[0], e_sem.at[0])

    took(pbuf, p_sem.at[0])


def shards(*args):
    tokens, gate, up, iproj, oproj, seg, lens, ainv, binv, query = args
    tc = gate.shape[0] // CHUNKS
    dma, vmem = pltpu.SemaphoreType.DMA, pltpu.VMEM
    return pl.pallas_call(
        kernel,
        out_shape=jax.ShapeDtypeStruct((4, 512), F32),
        in_specs=[pl.BlockSpec(memory_space=pl.ANY)] * 10,
        out_specs=pl.BlockSpec(memory_space=pltpu.VMEM),
        scratch_shapes=[
            vmem(tokens.shape, BF16),
            vmem(gate.shape, BF16),
            vmem(up.shape, BF16),
            vmem(iproj.shape, BF16),
            vmem(oproj.shape, BF16),
            vmem((1, 512), jnp.int32),
            vmem((1, 4), jnp.int32),
            vmem(ainv.shape, F32),
            vmem(binv.shape, F32),
            vmem(query.shape, F32),
            vmem((2, 32, 128), F32),
            vmem((8, 32, 128), F32),
            vmem((CHUNKS, 8, 16, tc), F32),
            vmem((CHUNKS, 7, 16, tc), F32),
            vmem((4, 256, 512), F32),
            vmem((2, 4, 128, 512), BF16),
            vmem((2, 4, 128, 512), BF16),
            vmem((32, 128), F32),
            vmem((32, 8, 128), F32),
            vmem((64, 512), F32),
            vmem((8, 4, 512), F32),
            vmem((7, 4, 512), F32),
            dma((8 + 2 * CHUNKS,)),
            dma((2,)),
            dma((CHUNKS,)),
            dma((CHUNKS,)),
            dma((6,)),
            dma((6,)),
            dma((2,)),
            dma((2,)),
            pltpu.SemaphoreType.REGULAR,
        ],
        compiler_params=pltpu.CompilerParams(
            collective_id=0, has_side_effects=True, vmem_limit_bytes=56 * 2**20
        ),
        cost_estimate=pl.CostEstimate(flops=10**9, bytes_accessed=12 * 10**6, transcendentals=0),
    )(tokens, gate, up, iproj, oproj, seg.reshape(1, 512), lens.reshape(1, 4), ainv, binv, query)


def solution(mesh):
    return jax.shard_map(
        shards,
        mesh=mesh,
        in_specs=(
            P(("dp", "tensor"), None),
            P("dp", "tensor"),
            P("dp", "tensor"),
            P(),
            P("tensor", None),
            P("dp"),
            P("dp"),
            P(),
            P(),
            P("tensor", "dp"),
        ),
        out_specs=P("dp", "tensor"),
        check_vma=False,
    )
```

```python
import jax
import jax.numpy as jnp
from jax import lax
from jax.experimental import pallas as pl
from jax.experimental.pallas import tpu as pltpu
from jax.sharding import PartitionSpec as P

F32, BF16 = jnp.float32, jnp.bfloat16
FAR_FIRST = (4, 3, 5, 2, 6, 1, 7)
PEERS = ((2, 1), (2, 0), (1, 1), (3, 1), (1, 0), (3, 0), (0, 1))
CHUNKS = 2
NN = (((1,), (0,)), ((), ()))
NT = (((1,), (1,)), ((), ()))


def mm(a, b, dims):
    return lax.dot_general(a, b, dims, preferred_element_type=F32)


def exact(a, b, dims):
    return lax.dot_general(a, b, dims, precision=lax.Precision.HIGHEST, preferred_element_type=F32)


def split(a):
    hi = a.astype(BF16)
    return hi, (a - hi.astype(F32)).astype(BF16)


def mm3(a, b, dims):
    (ah, al), (bh, bl) = a, b
    return mm(ah, bh, dims) + (mm(ah, bl, dims) + mm(al, bh, dims))


def iota(shape, axis):
    return lax.broadcasted_iota(jnp.int32, shape, axis)


def kernel(
    tokens_hbm, gate_hbm, up_hbm, iproj_hbm, oproj_hbm, seg_hbm, len_hbm, ainv_hbm, binv_hbm, query_hbm,
    out_ref,
    tokens, gate, up, iproj, oproj, seg, lens, ainv, binv, query,
    csend, cbuf, gsend, gbuf, qbuf, qhi, qlo, esend, ebuf, rsum, psend, pbuf,
    load_sem, c_sem, g_send, g_recv, q_send, q_recv, e_sem, p_sem, told, ready,
):
    d, z = lax.axis_index("dp"), lax.axis_index("tensor")
    y, x, c = d // 8, lax.rem(d // 2, 4), lax.rem(d, 2)
    m, jz = z // 4, lax.rem(z, 4)

    def dp(y_to, x_to, c_to):
        return lax.rem(y_to, 4) * 8 + lax.rem(x_to, 4) * 2 + lax.rem(c_to, 2)

    def ring(k):
        return lax.rem(z + k, 8)

    def send(src, dst, s_sem, r_sem, to):
        copy = pltpu.make_async_remote_copy(
            src_ref=src, dst_ref=dst, send_sem=s_sem, recv_sem=r_sem, device_id=to, device_id_type=pl.DeviceIdType.MESH
        )
        copy.start()

    def took(ref, sem):
        pltpu.make_async_copy(ref, ref, sem).wait()

    left, right = (dp(y, x + 3, c), z), (dp(y, x + 1, c), z)
    peers = [(dp(y + ky, x, c + kc), z) for ky, kc in PEERS]

    tc = gate.shape[0] // CHUNKS
    rows = [pl.ds(n * tc, tc) for n in range(CHUNKS)]
    pairs = [(query_hbm, query), (ainv_hbm, ainv), (binv_hbm, binv), (tokens_hbm, tokens), (iproj_hbm, iproj),
             (oproj_hbm, oproj), (seg_hbm, seg), (len_hbm, lens)]
    for n in range(CHUNKS):
        pairs += [(gate_hbm.at[rows[n]], gate.at[rows[n]]), (up_hbm.at[rows[n]], up.at[rows[n]])]
    loads = [pltpu.make_async_copy(src, dst, load_sem.at[i]) for i, (src, dst) in enumerate(pairs)]
    for load in loads:
        load.start()

    barrier = pltpu.get_barrier_semaphore()
    pair = (dp(y, x, c + 1), z)
    greet = [(dp(y, x, 0), ring(k)) for k in FAR_FIRST]
    greet += [(dp(y + k, x, 0), z) for k in (2, 1, 3)]
    greet += [(dp(y, x + k, 1), z) for k in (1, 3)] + [pair]

    def signal(sem, to):
        pl.semaphore_signal(sem, inc=1, device_id=to, device_id_type=pl.DeviceIdType.MESH)

    def learn(core, count):
        @pl.when(c == core)
        def _():
            pl.semaphore_wait(barrier, count)
            signal(told, pair)

        @pl.when(c != core)
        def _():
            pl.semaphore_wait(told, 1)

    for to in greet:
        signal(barrier, to)

    loads[1].wait()
    r, i = iota((64, 64), 0), iota((64, 64), 1)
    source = (((r >> 2) & 1) << 5) + ((r & 1) << 4) + (((r >> 5) & 1) << 3) + (((r >> 1) & 1) << 2) + ((r >> 3) & 3)
    order = (source == i).astype(F32)
    halves = [(iota((64, 128), 1) == iota((64, 128), 0) + 64 * n).astype(F32) for n in range(2)]
    left_inverse = split(
        jnp.concatenate([exact(exact(order, ainv[n], NN), halves[n], NN) for n in range(2)], axis=0)
    )
    loads[2].wait()
    right_inverse = split(jnp.concatenate([exact(binv[n], halves[n], NN) for n in range(2)], axis=0))

    loads[3].wait()
    loads[4].wait()
    codes = mm(tokens[...], iproj[...], NN)
    both = mm3(left_inverse, split(jnp.concatenate([codes, codes], axis=0)), NT)
    low = iota((32, 128), 1) < 64
    for n in range(2):
        csend[n] = jnp.where(low, both[64 * n : 64 * n + 32], both[64 * n + 32 : 64 * n + 64])
    cbuf[z] = csend[m]

    r, i = iota((256, 256), 0), iota((256, 256), 1)
    shuffle = ((((r >> 4) & 3) << 6) + ((r >> 6) << 4) + (r & 15) == i).astype(BF16)
    loads[0].wait()
    q_hi, q_lo = split(query[...])
    qbuf[x] = mm(shuffle, q_hi, NT) + mm(shuffle, q_lo, NT)

    learn(1, 5)
    first, second = pl.ds(0, 128), pl.ds(128, 128)
    send(qbuf.at[x, first], qbuf.at[x, first], q_send.at[0], q_recv.at[0], left)
    send(qbuf.at[x, second], qbuf.at[x, second], q_send.at[1], q_recv.at[1], right)
    send(qbuf.at[x, second], qbuf.at[x, second], q_send.at[2], q_recv.at[2], left)
    send(qbuf.at[x, first], qbuf.at[x, first], q_send.at[3], q_recv.at[3], right)

    learn(0, 21)
    for k in FAR_FIRST:
        send(csend.at[ring(k) // 4], cbuf.at[z], c_sem.at[0], c_sem.at[1], (d, ring(k)))

    loads[5].wait()
    low = iota((tc, 128), 1) < 64
    for n in range(CHUNKS):
        loads[8 + 2 * n].wait()
        part = mm(gate[rows[n]], oproj[...], NN)
        loads[9 + 2 * n].wait()
        part = jnp.where(low, part, mm(up[rows[n]], oproj[...], NN))
        gsend[n] = mm3(right_inverse, split(part), NT).reshape(8, 16, tc)
        for k in FAR_FIRST:
            send(gsend.at[n, ring(k)], gbuf.at[n, k - 1], g_send.at[n], g_recv.at[n], (d, ring(k)))

    for to in peers:
        signal(ready, to)

    loads[6].wait()
    loads[7].wait()
    weights = [
        jnp.where(seg[...] == g, 1.0 / jnp.broadcast_to(lens[:, g : g + 1], seg.shape).astype(F32), 0.0) for g in range(4)
    ]

    took(cbuf.at[pl.ds(0, 7)], c_sem.at[1])
    low = iota((32, 128), 1) < 64
    upper, lower = [], []
    for n in range(4):
        even, odd = cbuf[2 * n], cbuf[2 * n + 1]
        upper.append(jnp.where(low, even, pltpu.roll(odd, 64, 1)))
        lower.append(jnp.where(low, pltpu.roll(even, 64, 1), odd))
    codes_t = split(jnp.concatenate([jnp.concatenate(upper, axis=1), jnp.concatenate(lower, axis=1)], axis=0))

    took(qbuf.at[0, first], q_recv.at[0])
    after = lax.rem(x + 1, 4)
    send(qbuf.at[after, first], qbuf.at[after, first], q_send.at[4], q_recv.at[4], left)
    took(qbuf.at[0, first], q_recv.at[1])
    before = lax.rem(x + 3, 4)
    send(qbuf.at[before, second], qbuf.at[before, second], q_send.at[5], q_recv.at[5], right)

    sums = []
    for n in range(CHUNKS):
        took(gbuf.at[n], g_recv.at[n])
        total = gsend[n, z]
        for k in range(7):
            total = total + gbuf[n, k]
        sums.append(total)
    columns = jnp.concatenate(sums, axis=1)
    spread = jnp.concatenate([columns * w for w in weights] * 2, axis=0)
    outer = mm3(codes_t, split(spread), NT)
    turned = [outer] + [pltpu.roll(outer, 16 * k, 1) for k in (1, 2, 3)]
    place = iota((8, 128), 1) >> 4
    for g in range(4):
        piece = turned[(0 - g) % 4][0:8]
        for k in range(1, 8):
            piece = jnp.where(place == k, turned[(k - g) % 4][8 * k : 8 * k + 8], piece)
        esend[pl.ds(g, 8, stride=4), :] = piece

    pl.semaphore_wait(ready, len(peers))
    mine = [[(y == 2 * m + ky) & (c == kc) for kc in range(2)] for ky in range(2)]
    for k in FAR_FIRST + (0,):
        for ky in range(2):
            for kc in range(2):
                y_to, src = 2 * m + ky, esend.at[pl.ds(8 * (2 * ky + kc), 8)]
                slot = (lax.rem(y - y_to + 4, 4) * 2 + lax.rem(c + kc, 2)) * 4 + jz
                dst = ebuf.at[slot]
                to = (dp(y_to, x, kc), ring(k))
                if k:
                    send(src, dst, e_sem.at[0], e_sem.at[1], to)
                else:

                    @pl.when(jnp.logical_not(mine[ky][kc]))
                    def _(src=src, dst=dst, to=to):
                        send(src, dst, e_sem.at[0], e_sem.at[1], to)

                    @pl.when(mine[ky][kc])
                    def _(src=src, dst=dst):
                        pltpu.make_async_copy(src, dst, e_sem.at[1]).start()

    def prepare(block, jzs):
        for n in jzs:
            hi, lo = split(qbuf[block, pl.ds(64 * n, 64)])
            at = pl.ds(pl.multiple_of(lax.rem(block, 2) * 64, 64), 64)
            qhi[block // 2, n, at] = hi
            qlo[block // 2, n, at] = lo

    prepare(x, range(4))
    prepare(after, range(2))
    prepare(before, range(2, 4))
    took(qbuf.at[0, first], q_recv.at[2])
    prepare(after, range(2, 4))
    took(qbuf.at[0, first], q_recv.at[3])
    prepare(before, range(2))
    beyond = lax.rem(x + 2, 4)
    took(qbuf.at[0, first], q_recv.at[4])
    prepare(beyond, range(2))
    took(qbuf.at[0, first], q_recv.at[5])
    prepare(beyond, range(2, 4))

    took(ebuf, e_sem.at[1])
    pieces = ebuf[...].reshape(8, 4, 8, 128)
    e_hi, e_lo = split(jnp.concatenate([pieces[:, n].reshape(64, 128) for n in range(4)], axis=1))
    e_both = jnp.concatenate([e_hi, e_lo], axis=0)
    part = []
    for n in range(2):
        main = mm(e_both, qhi[n].reshape(512, 512), NN)
        part.append(main[:64] + main[64:] + mm(e_hi, qlo[n].reshape(512, 512), NN))
    rsum[...] = part[1]
    for n in range(8):
        psend[n] = part[0][8 * n : 8 * n + 4] + rsum[8 * n + 4 : 8 * n + 8]
    for (ky, kc), to in zip(PEERS, peers, strict=True):
        n = 2 * ky + kc
        send(psend.at[n], pbuf.at[n - 1], p_sem.at[0], p_sem.at[1], to)
    took(pbuf, p_sem.at[1])
    total = psend[0]
    for n in range(7):
        total = total + pbuf[n]
    out_ref[...] = total

    took(cbuf.at[pl.ds(0, 7)], c_sem.at[0])
    for n in range(CHUNKS):
        took(gbuf.at[n], g_send.at[n])
    for n in range(6):
        took(qbuf.at[0, first], q_send.at[n])
    took(ebuf.at[pl.ds(0, 31)], e_sem.at[0])

    @pl.when(m != y // 2)
    def _():
        took(ebuf.at[0], e_sem.at[0])

    took(pbuf, p_sem.at[0])


def shards(*args):
    tokens, gate, up, iproj, oproj, seg, lens, ainv, binv, query = args
    tc = gate.shape[0] // CHUNKS
    dma, vmem = pltpu.SemaphoreType.DMA, pltpu.VMEM
    return pl.pallas_call(
        kernel,
        out_shape=jax.ShapeDtypeStruct((4, 512), F32),
        in_specs=[pl.BlockSpec(memory_space=pl.ANY)] * 10,
        out_specs=pl.BlockSpec(memory_space=pltpu.VMEM),
        scratch_shapes=[
            vmem(tokens.shape, BF16),
            vmem(gate.shape, BF16),
            vmem(up.shape, BF16),
            vmem(iproj.shape, BF16),
            vmem(oproj.shape, BF16),
            vmem((1, 512), jnp.int32),
            vmem((1, 4), jnp.int32),
            vmem(ainv.shape, F32),
            vmem(binv.shape, F32),
            vmem(query.shape, F32),
            vmem((2, 32, 128), F32),
            vmem((8, 32, 128), F32),
            vmem((CHUNKS, 8, 16, tc), F32),
            vmem((CHUNKS, 7, 16, tc), F32),
            vmem((4, 256, 512), F32),
            vmem((2, 4, 128, 512), BF16),
            vmem((2, 4, 128, 512), BF16),
            vmem((32, 128), F32),
            vmem((32, 8, 128), F32),
            vmem((64, 512), F32),
            vmem((8, 4, 512), F32),
            vmem((7, 4, 512), F32),
            dma((8 + 2 * CHUNKS,)),
            dma((2,)),
            dma((CHUNKS,)),
            dma((CHUNKS,)),
            dma((6,)),
            dma((6,)),
            dma((2,)),
            dma((2,)),
            pltpu.SemaphoreType.REGULAR,
            pltpu.SemaphoreType.REGULAR,
        ],
        compiler_params=pltpu.CompilerParams(
            collective_id=0, has_side_effects=True, vmem_limit_bytes=56 * 2**20
        ),
        cost_estimate=pl.CostEstimate(flops=10**9, bytes_accessed=12 * 10**6, transcendentals=0),
    )(tokens, gate, up, iproj, oproj, seg.reshape(1, 512), lens.reshape(1, 4), ainv, binv, query)


def solution(mesh):
    return jax.shard_map(
        shards,
        mesh=mesh,
        in_specs=(
            P(("dp", "tensor"), None),
            P("dp", "tensor"),
            P("dp", "tensor"),
            P(),
            P("tensor", None),
            P("dp"),
            P("dp"),
            P(),
            P(),
            P("tensor", "dp"),
        ),
        out_specs=P("dp", "tensor"),
        check_vma=False,
    )
```

```python
import jax
import jax.numpy as jnp
from jax import lax
from jax.experimental import pallas as pl
from jax.experimental.pallas import tpu as pltpu
from jax.sharding import PartitionSpec as P

F32, BF16 = jnp.float32, jnp.bfloat16
FAR_FIRST = (4, 3, 5, 2, 6, 1, 7)
PEERS = ((2, 1), (2, 0), (1, 1), (3, 1), (1, 0), (3, 0), (0, 1))
CHUNKS = 2
NN = (((1,), (0,)), ((), ()))
NT = (((1,), (1,)), ((), ()))


def mm(a, b, dims):
    return lax.dot_general(a, b, dims, preferred_element_type=F32)


def exact(a, b, dims):
    return lax.dot_general(a, b, dims, precision=lax.Precision.HIGHEST, preferred_element_type=F32)


def split(a):
    hi = a.astype(BF16)
    return hi, (a - hi.astype(F32)).astype(BF16)


def mm3(a, b, dims):
    (ah, al), (bh, bl) = a, b
    return mm(ah, bh, dims) + (mm(ah, bl, dims) + mm(al, bh, dims))


def iota(shape, axis):
    return lax.broadcasted_iota(jnp.int32, shape, axis)


def kernel(
    tokens_hbm, gate_hbm, up_hbm, iproj_hbm, oproj_hbm, seg_hbm, len_hbm, ainv_hbm, binv_hbm, query_hbm,
    out_ref,
    tokens, gate, up, iproj, oproj, seg, lens, ainv, binv, query,
    csend, cbuf, gsend, gbuf, qbuf, qhi, qlo, esend, ebuf, rsum, psend, pbuf,
    load_sem, c_sem, g_send, g_recv, q_send, q_recv, e_sem, p_sem, told, ready,
):
    d, z = lax.axis_index("dp"), lax.axis_index("tensor")
    y, x, c = d // 8, lax.rem(d // 2, 4), lax.rem(d, 2)
    m, jz = z // 4, lax.rem(z, 4)

    def dp(y_to, x_to, c_to):
        return lax.rem(y_to, 4) * 8 + lax.rem(x_to, 4) * 2 + lax.rem(c_to, 2)

    def ring(k):
        return lax.rem(z + k, 8)

    def send(src, dst, s_sem, r_sem, to):
        copy = pltpu.make_async_remote_copy(
            src_ref=src, dst_ref=dst, send_sem=s_sem, recv_sem=r_sem, device_id=to, device_id_type=pl.DeviceIdType.MESH
        )
        copy.start()

    def took(ref, sem):
        pltpu.make_async_copy(ref, ref, sem).wait()

    left, right = (dp(y, x + 3, c), z), (dp(y, x + 1, c), z)
    peers = [(dp(y + ky, x, c + kc), z) for ky, kc in PEERS]

    tc = gate.shape[0] // CHUNKS
    rows = [pl.ds(n * tc, tc) for n in range(CHUNKS)]
    pairs = [(query_hbm, query), (ainv_hbm, ainv), (binv_hbm, binv), (tokens_hbm, tokens), (iproj_hbm, iproj), (oproj_hbm, oproj), (seg_hbm, seg), (len_hbm, lens), (gate_hbm.at[rows[0]], gate.at[rows[0]]), (up_hbm.at[rows[0]], up.at[rows[0]]), (gate_hbm.at[rows[1]], gate.at[rows[1]]), (up_hbm.at[rows[1]], up.at[rows[1]])]
    loads = [pltpu.make_async_copy(src, dst, load_sem.at[i]) for i, (src, dst) in enumerate(pairs)]
    for i in (0, 1, 2, 3, 4, 5, 6, 7, 8, 9, 10, 11):
        loads[i].start()

    barrier = pltpu.get_barrier_semaphore()
    pair = (dp(y, x, c + 1), z)
    greet = [(dp(y, x, 0), ring(k)) for k in FAR_FIRST]
    greet += [(dp(y + k, x, 0), z) for k in (2, 1, 3)]
    greet += [(dp(y, x + k, 1), z) for k in (1, 3)] + [pair]

    def signal(sem, to):
        pl.semaphore_signal(sem, inc=1, device_id=to, device_id_type=pl.DeviceIdType.MESH)

    def learn(core, count):
        @pl.when(c == core)
        def _():
            pl.semaphore_wait(barrier, count)
            signal(told, pair)

        @pl.when(c != core)
        def _():
            pl.semaphore_wait(told, 1)

    for to in greet:
        signal(barrier, to)

    loads[1].wait()
    r, i = iota((64, 64), 0), iota((64, 64), 1)
    source = (((r >> 2) & 1) << 5) + ((r & 1) << 4) + (((r >> 5) & 1) << 3) + (((r >> 1) & 1) << 2) + ((r >> 3) & 3)
    order = (source == i).astype(F32)
    halves = [(iota((64, 128), 1) == iota((64, 128), 0) + 64 * n).astype(F32) for n in range(2)]
    left_inverse = split(
        jnp.concatenate([exact(exact(order, ainv[n], NN), halves[n], NN) for n in range(2)], axis=0)
    )
    loads[2].wait()
    right_inverse = split(jnp.concatenate([exact(binv[n], halves[n], NN) for n in range(2)], axis=0))

    loads[3].wait()
    loads[4].wait()
    codes = mm(tokens[...], iproj[...], NN)
    both = mm3(left_inverse, split(jnp.concatenate([codes, codes], axis=0)), NT)
    low = iota((32, 128), 1) < 64
    for n in range(2):
        csend[n] = jnp.where(low, both[64 * n : 64 * n + 32], both[64 * n + 32 : 64 * n + 64])
    cbuf[z] = csend[m]

    r, i = iota((256, 256), 0), iota((256, 256), 1)
    shuffle = ((((r >> 4) & 3) << 6) + ((r >> 6) << 4) + (r & 15) == i).astype(BF16)
    loads[0].wait()
    q_hi, q_lo = split(query[...])
    qbuf[x] = mm(shuffle, q_hi, NT) + mm(shuffle, q_lo, NT)

    learn(1, 5)
    first, second = pl.ds(0, 128), pl.ds(128, 128)
    send(qbuf.at[x, first], qbuf.at[x, first], q_send.at[0], q_recv.at[0], left)
    send(qbuf.at[x, second], qbuf.at[x, second], q_send.at[1], q_recv.at[1], right)
    send(qbuf.at[x, second], qbuf.at[x, second], q_send.at[2], q_recv.at[2], left)
    send(qbuf.at[x, first], qbuf.at[x, first], q_send.at[3], q_recv.at[3], right)

    learn(0, 21)
    for k in FAR_FIRST:
        send(csend.at[ring(k) // 4], cbuf.at[z], c_sem.at[0], c_sem.at[1], (d, ring(k)))

    loads[5].wait()
    low = iota((tc, 128), 1) < 64
    for n in range(CHUNKS):
        loads[8 + 2 * n].wait()
        part = mm(gate[rows[n]], oproj[...], NN)
        loads[9 + 2 * n].wait()
        part = jnp.where(low, part, mm(up[rows[n]], oproj[...], NN))
        gsend[n] = mm3(right_inverse, split(part), NT).reshape(8, 16, tc)
        for k in FAR_FIRST:
            send(gsend.at[n, ring(k)], gbuf.at[n, k - 1], g_send.at[n], g_recv.at[n], (d, ring(k)))

    for to in peers:
        signal(ready, to)

    loads[6].wait()
    loads[7].wait()
    weights = [
        jnp.where(seg[...] == g, 1.0 / jnp.broadcast_to(lens[:, g : g + 1], seg.shape).astype(F32), 0.0) for g in range(4)
    ]

    took(cbuf.at[pl.ds(0, 7)], c_sem.at[1])
    low = iota((32, 128), 1) < 64
    upper, lower = [], []
    for n in range(4):
        even, odd = cbuf[2 * n], cbuf[2 * n + 1]
        upper.append(jnp.where(low, even, pltpu.roll(odd, 64, 1)))
        lower.append(jnp.where(low, pltpu.roll(even, 64, 1), odd))
    codes_t = split(jnp.concatenate([jnp.concatenate(upper, axis=1), jnp.concatenate(lower, axis=1)], axis=0))

    took(qbuf.at[0, first], q_recv.at[0])
    after = lax.rem(x + 1, 4)
    send(qbuf.at[after, first], qbuf.at[after, first], q_send.at[4], q_recv.at[4], left)
    took(qbuf.at[0, first], q_recv.at[1])
    before = lax.rem(x + 3, 4)
    send(qbuf.at[before, second], qbuf.at[before, second], q_send.at[5], q_recv.at[5], right)

    sums = []
    for n in range(CHUNKS):
        took(gbuf.at[n], g_recv.at[n])
        total = gsend[n, z]
        for k in range(7):
            total = total + gbuf[n, k]
        sums.append(total)
    columns = jnp.concatenate(sums, axis=1)
    spread = jnp.concatenate([columns * w for w in weights] * 2, axis=0)
    outer = mm3(codes_t, split(spread), NT)
    turned = [outer] + [pltpu.roll(outer, 16 * k, 1) for k in (1, 2, 3)]
    place = iota((8, 128), 1) >> 4
    for g in range(4):
        piece = turned[(0 - g) % 4][0:8]
        for k in range(1, 8):
            piece = jnp.where(place == k, turned[(k - g) % 4][8 * k : 8 * k + 8], piece)
        esend[pl.ds(g, 8, stride=4), :] = piece

    pl.semaphore_wait(ready, len(peers))
    mine = [[(y == 2 * m + ky) & (c == kc) for kc in range(2)] for ky in range(2)]
    for zt in (0, 1, 2, 3, 7, 4, 6, 5):
        for ky in range(2):
            for kc in range(2):
                y_to, src = 2 * m + ky, esend.at[pl.ds(8 * (2 * ky + kc), 8)]
                slot = (lax.rem(y - y_to + 4, 4) * 2 + lax.rem(c + kc, 2)) * 4 + jz
                dst = ebuf.at[slot]
                own = mine[ky][kc] & (z == zt)

                @pl.when(jnp.logical_not(own))
                def _(src=src, dst=dst, to=(dp(y_to, x, kc), zt)):
                    send(src, dst, e_sem.at[0], e_sem.at[1], to)

                @pl.when(own)
                def _(src=src, dst=dst):
                    pltpu.make_async_copy(src, dst, e_sem.at[1]).start()

    def prepare(block, jzs):
        for n in jzs:
            hi, lo = split(qbuf[block, pl.ds(64 * n, 64)])
            at = pl.ds(pl.multiple_of(lax.rem(block, 2) * 64, 64), 64)
            qhi[block // 2, n, at] = hi
            qlo[block // 2, n, at] = lo

    prepare(x, range(4))
    prepare(after, range(2))
    prepare(before, range(2, 4))
    took(qbuf.at[0, first], q_recv.at[2])
    prepare(after, range(2, 4))
    took(qbuf.at[0, first], q_recv.at[3])
    prepare(before, range(2))
    beyond = lax.rem(x + 2, 4)
    took(qbuf.at[0, first], q_recv.at[4])
    prepare(beyond, range(2))
    took(qbuf.at[0, first], q_recv.at[5])
    prepare(beyond, range(2, 4))

    took(ebuf, e_sem.at[1])
    pieces = ebuf[...].reshape(8, 4, 8, 128)
    e_hi, e_lo = split(jnp.concatenate([pieces[:, n].reshape(64, 128) for n in range(4)], axis=1))
    e_both = jnp.concatenate([e_hi, e_lo], axis=0)
    part = []
    for n in range(2):
        main = mm(e_both, qhi[n].reshape(512, 512), NN)
        part.append(main[:64] + main[64:] + mm(e_hi, qlo[n].reshape(512, 512), NN))
    rsum[...] = part[1]
    for n in range(8):
        psend[n] = part[0][8 * n : 8 * n + 4] + rsum[8 * n + 4 : 8 * n + 8]
    for (ky, kc), to in zip(PEERS, peers, strict=True):
        n = 2 * ky + kc
        send(psend.at[n], pbuf.at[n - 1], p_sem.at[0], p_sem.at[1], to)
    took(pbuf, p_sem.at[1])
    total = psend[0]
    for n in range(7):
        total = total + pbuf[n]
    out_ref[...] = total

    took(cbuf.at[pl.ds(0, 7)], c_sem.at[0])
    for n in range(CHUNKS):
        took(gbuf.at[n], g_send.at[n])
    for n in range(6):
        took(qbuf.at[0, first], q_send.at[n])
    took(ebuf.at[pl.ds(0, 31)], e_sem.at[0])

    @pl.when(m != y // 2)
    def _():
        took(ebuf.at[0], e_sem.at[0])

    took(pbuf, p_sem.at[0])


def shards(*args):
    tokens, gate, up, iproj, oproj, seg, lens, ainv, binv, query = args
    tc = gate.shape[0] // CHUNKS
    dma, vmem = pltpu.SemaphoreType.DMA, pltpu.VMEM
    return pl.pallas_call(
        kernel,
        out_shape=pltpu.VMEM((4, 512), F32),
        in_specs=[pl.BlockSpec(memory_space=pl.ANY)] * 10,
        out_specs=pl.BlockSpec(memory_space=pltpu.VMEM),
        scratch_shapes=[
            vmem(tokens.shape, BF16),
            vmem(gate.shape, BF16),
            vmem(up.shape, BF16),
            vmem(iproj.shape, BF16),
            vmem(oproj.shape, BF16),
            vmem((1, 512), jnp.int32),
            vmem((1, 4), jnp.int32),
            vmem(ainv.shape, F32),
            vmem(binv.shape, F32),
            vmem(query.shape, F32),
            vmem((2, 32, 128), F32),
            vmem((8, 32, 128), F32),
            vmem((CHUNKS, 8, 16, tc), F32),
            vmem((CHUNKS, 7, 16, tc), F32),
            vmem((4, 256, 512), F32),
            vmem((2, 4, 128, 512), BF16),
            vmem((2, 4, 128, 512), BF16),
            vmem((32, 128), F32),
            vmem((32, 8, 128), F32),
            vmem((64, 512), F32),
            vmem((8, 4, 512), F32),
            vmem((7, 4, 512), F32),
            dma((8 + 2 * CHUNKS,)),
            dma((2,)),
            dma((CHUNKS,)),
            dma((CHUNKS,)),
            dma((6,)),
            dma((6,)),
            dma((2,)),
            dma((2,)),
            pltpu.SemaphoreType.REGULAR,
            pltpu.SemaphoreType.REGULAR,
        ],
        compiler_params=pltpu.CompilerParams(
            collective_id=0, has_side_effects=True, vmem_limit_bytes=56 * 2**20
        ),
        cost_estimate=pl.CostEstimate(flops=10**9, bytes_accessed=12 * 10**6, transcendentals=0),
    )(tokens, gate, up, iproj, oproj, seg.reshape(1, 512), lens.reshape(1, 4), ainv, binv, query)


def solution(mesh):
    return jax.shard_map(
        shards,
        mesh=mesh,
        in_specs=(
            P(("dp", "tensor"), None),
            P("dp", "tensor"),
            P("dp", "tensor"),
            P(),
            P("tensor", None),
            P("dp"),
            P("dp"),
            P(),
            P(),
            P("tensor", "dp"),
        ),
        out_specs=P("dp", "tensor"),
        check_vma=False,
    )
```

```python
import jax
import jax.numpy as jnp
from jax import lax
from jax.experimental import pallas as pl
from jax.experimental.pallas import tpu as pltpu
from jax.sharding import PartitionSpec as P

F32, BF16 = jnp.float32, jnp.bfloat16
FAR_FIRST = (4, 3, 5, 2, 6, 1, 7)
PEERS = (2, 1, 3)
CHUNKS = 2
NN = (((1,), (0,)), ((), ()))
NT = (((1,), (1,)), ((), ()))


def mm(a, b, dims):
    return lax.dot_general(a, b, dims, preferred_element_type=F32)


def exact(a, b, dims):
    return lax.dot_general(a, b, dims, precision=lax.Precision.HIGHEST, preferred_element_type=F32)


def split(a):
    hi = a.astype(BF16)
    return hi, (a - hi.astype(F32)).astype(BF16)


def mm3(a, b, dims):
    (ah, al), (bh, bl) = a, b
    return mm(ah, bh, dims) + (mm(ah, bl, dims) + mm(al, bh, dims))


def iota(shape, axis):
    return lax.broadcasted_iota(jnp.int32, shape, axis)


def kernel(
    tokens_hbm, gate_hbm, up_hbm, iproj_hbm, oproj_hbm, seg_hbm, len_hbm, ainv_hbm, binv_hbm, query_hbm,
    out_ref,
    tokens, gate, up, iproj, oproj, seg, lens, ainv, binv, query,
    csend, cbuf, gsend, gbuf, qbuf, qhi, qlo, esend, ebuf, rsum, psend, pbuf,
    load_sem, c_sem, g_send, g_recv, q_send, q_recv, e_sem, p_sem, told, ready,
):
    d, z = lax.axis_index("dp"), lax.axis_index("tensor")
    y, x, c = d // 8, lax.rem(d // 2, 4), lax.rem(d, 2)
    m, jz = z // 4, lax.rem(z, 4)

    def dp(y_to, x_to, c_to):
        return lax.rem(y_to, 4) * 8 + lax.rem(x_to, 4) * 2 + lax.rem(c_to, 2)

    def ring(k):
        return lax.rem(z + k, 8)

    def send(src, dst, s_sem, r_sem, to):
        copy = pltpu.make_async_remote_copy(
            src_ref=src, dst_ref=dst, send_sem=s_sem, recv_sem=r_sem, device_id=to, device_id_type=pl.DeviceIdType.MESH
        )
        copy.start()

    def took(ref, sem):
        pltpu.make_async_copy(ref, ref, sem).wait()

    left, right = (dp(y, x + 3, c), z), (dp(y, x + 1, c), z)
    peers = [(dp(y + k, x, c), z) for k in PEERS]

    tc = gate.shape[0] // CHUNKS
    rows = [pl.ds(n * tc, tc) for n in range(CHUNKS)]
    pairs = [(query_hbm, query), (ainv_hbm, ainv), (binv_hbm, binv), (tokens_hbm, tokens), (iproj_hbm, iproj),
             (oproj_hbm, oproj), (seg_hbm, seg), (len_hbm, lens)]
    for n in range(CHUNKS):
        pairs += [(gate_hbm.at[rows[n]], gate.at[rows[n]]), (up_hbm.at[rows[n]], up.at[rows[n]])]
    loads = [pltpu.make_async_copy(src, dst, load_sem.at[i]) for i, (src, dst) in enumerate(pairs)]
    for load in loads:
        load.start()

    barrier = pltpu.get_barrier_semaphore()
    pair = (dp(y, x, c + 1), z)
    greet = [(dp(y, x, 1), ring(k)) for k in FAR_FIRST]
    greet += [(dp(y + k, x, 1), z) for k in PEERS]
    greet += [(dp(y, x + k, 0), z) for k in (1, 3)] + [pair]

    def signal(sem, to):
        pl.semaphore_signal(sem, inc=1, device_id=to, device_id_type=pl.DeviceIdType.MESH)

    def learn(core, count):
        @pl.when(c == core)
        def _():
            pl.semaphore_wait(barrier, count)
            signal(told, pair)

        @pl.when(c != core)
        def _():
            pl.semaphore_wait(told, 1)

    for to in greet:
        signal(barrier, to)

    first, second = pl.ds(0, 128), pl.ds(128, 128)

    def pass_queries(block, half, i, to):
        ref = qbuf.at[block, c, half]
        send(ref, ref, q_send.at[i], q_recv.at[i], to)

    def took_queries(i):
        took(qbuf.at[0, 0, first], q_recv.at[i])

    def share_queries():
        r, i = iota((256, 256), 0), iota((256, 256), 1)
        shuffle = ((((r >> 4) & 3) << 6) + ((r >> 6) << 4) + (r & 15) == i).astype(BF16)
        loads[0].wait()
        q_hi, q_lo = split(query[...])
        qbuf[x, c] = mm(shuffle, q_hi, NT) + mm(shuffle, q_lo, NT)

        learn(0, 5)
        pass_queries(x, first, 0, left)
        pass_queries(x, second, 1, right)
        pass_queries(x, second, 2, left)
        pass_queries(x, first, 3, right)
        pass_queries(x, first, 6, pair)
        pass_queries(x, second, 7, pair)

    @pl.when(z < 4)
    def _():
        share_queries()

    loads[1].wait()
    r, i = iota((64, 64), 0), iota((64, 64), 1)
    source = (((r >> 2) & 1) << 5) + ((r & 3) << 3) + (r >> 3)
    order = (source == i).astype(F32)
    halves = [(iota((64, 128), 1) == iota((64, 128), 0) + 64 * n).astype(F32) for n in range(2)]
    left_inverse = split(
        jnp.concatenate([exact(exact(order, ainv[n], NN), halves[n], NN) for n in range(2)], axis=0)
    )
    loads[2].wait()
    right_inverse = split(jnp.concatenate([exact(binv[n], halves[n], NN) for n in range(2)], axis=0))

    @pl.when(z >= 4)
    def _():
        share_queries()

    loads[3].wait()
    loads[4].wait()
    codes = mm(tokens[...], iproj[...], NN)
    both = mm3(left_inverse, split(jnp.concatenate([codes, codes], axis=0)), NT)
    low = iota((32, 128), 1) < 64
    for n in range(2):
        csend[n] = jnp.where(low, both[64 * n : 64 * n + 32], both[64 * n + 32 : 64 * n + 64])
    cbuf[z] = csend[m]

    learn(1, 21)
    for k in FAR_FIRST:
        send(csend.at[ring(k) // 4], cbuf.at[z], c_sem.at[0], c_sem.at[1], (d, ring(k)))

    loads[5].wait()
    low = iota((tc, 128), 1) < 64
    for n in range(CHUNKS):
        loads[8 + 2 * n].wait()
        part = mm(gate[rows[n]], oproj[...], NN)
        loads[9 + 2 * n].wait()
        part = jnp.where(low, part, mm(up[rows[n]], oproj[...], NN))
        gsend[n] = mm3(right_inverse, split(part), NT).reshape(8, 16, tc)
        for k in FAR_FIRST:
            send(gsend.at[n, ring(k)], gbuf.at[n, k - 1], g_send.at[n], g_recv.at[n], (d, ring(k)))

    for to in peers:
        signal(ready, to)

    loads[6].wait()
    loads[7].wait()
    weights = [
        jnp.where(seg[...] == g, 1.0 / jnp.broadcast_to(lens[:, g : g + 1], seg.shape).astype(F32), 0.0) for g in range(4)
    ]

    took(cbuf.at[pl.ds(0, 7)], c_sem.at[1])
    low = iota((32, 128), 1) < 64
    upper, lower = [], []
    for n in range(4):
        even, odd = cbuf[2 * n], cbuf[2 * n + 1]
        upper.append(jnp.where(low, even, pltpu.roll(odd, 64, 1)))
        lower.append(jnp.where(low, pltpu.roll(even, 64, 1), odd))
    codes_t = split(jnp.concatenate([jnp.concatenate(upper, axis=1), jnp.concatenate(lower, axis=1)], axis=0))

    after, before, beyond = lax.rem(x + 1, 4), lax.rem(x + 3, 4), lax.rem(x + 2, 4)
    took_queries(0)
    pass_queries(after, first, 4, left)
    pass_queries(after, first, 8, pair)
    took_queries(1)
    pass_queries(before, second, 5, right)
    pass_queries(before, second, 9, pair)

    pl.semaphore_wait(ready, len(peers))

    outer = 0.0
    for n in range(CHUNKS):
        took(gbuf.at[n], g_recv.at[n])
        total = ((gsend[n, z] + gbuf[n, 0]) + (gbuf[n, 1] + gbuf[n, 2])) + ((gbuf[n, 3] + gbuf[n, 4]) + (gbuf[n, 5] + gbuf[n, 6]))
        at = slice(n * tc, (n + 1) * tc)
        hi, lo = split(jnp.concatenate([total * w[:, at] for w in weights], axis=0))
        hi, lo = jnp.concatenate([hi, hi], axis=0), jnp.concatenate([lo, lo], axis=0)
        c_hi, c_lo = codes_t[0][:, at], codes_t[1][:, at]
        outer = outer + mm(jnp.concatenate([c_hi, c_lo, c_hi], axis=1), jnp.concatenate([hi, hi, lo], axis=1), NT)
    turned = [outer] + [pltpu.roll(outer, 16 * k, 1) for k in (1, 2, 3)]
    place = iota((8, 128), 1) >> 4
    for g in range(4):
        piece = turned[(0 - g) % 4][0:8]
        for k in range(1, 8):
            piece = jnp.where(place == k, turned[(k - g) % 4][8 * k : 8 * k + 8], piece)
        esend[pl.ds(g, 8, stride=4), :] = piece

    for k in FAR_FIRST + (0,):
        for n in range(2):
            y_to = 2 * m + n
            src = esend.at[pl.ds(16 * n, 16)]
            dst = ebuf.at[lax.rem(y - y_to + 4, 4) * 4 + jz]
            to = (dp(y_to, x, c), ring(k))
            if k:
                send(src, dst, e_sem.at[0], e_sem.at[1], to)
            else:

                @pl.when(y != y_to)
                def _(src=src, dst=dst, to=to):
                    send(src, dst, e_sem.at[0], e_sem.at[1], to)

                @pl.when(y == y_to)
                def _(src=src, dst=dst):
                    pltpu.make_async_copy(src, dst, e_sem.at[1]).start()

    def prepare(block, core, half):
        for n in (0, 1) if half is first else (2, 3):
            hi, lo = split(qbuf[block, core, pl.ds(64 * n, 64)])
            at = pl.ds(pl.multiple_of(core * 64, 64), 64)
            qhi[block, n, at] = hi
            qlo[block, n, at] = lo

    took_queries(2)
    pass_queries(after, second, 10, pair)
    took_queries(3)
    pass_queries(before, first, 11, pair)
    for block, half in ((x, first), (x, second), (after, first), (before, second), (after, second), (before, first)):
        prepare(block, c, half)
    took_queries(4)
    pass_queries(beyond, first, 12, pair)
    took_queries(5)
    pass_queries(beyond, second, 13, pair)
    prepare(beyond, c, first)
    prepare(beyond, c, second)
    for n, (block, half) in enumerate(
        ((x, first), (x, second), (after, first), (before, second), (after, second), (before, first), (beyond, first), (beyond, second))
    ):
        took_queries(6 + n)
        prepare(block, 1 - c, half)

    took(ebuf, e_sem.at[1])
    pieces = ebuf[...].reshape(4, 4, 16, 128)
    e_hi, e_lo = split(jnp.concatenate([pieces[:, n].reshape(64, 128) for n in range(4)], axis=1))
    e_both = jnp.concatenate([e_hi, e_lo], axis=0)
    for n in range(4):
        main = mm(e_both, qhi[n].reshape(512, 512), NN)
        rsum[n] = main[:64] + main[64:] + mm(e_hi, qlo[n].reshape(512, 512), NN)
    for n in (2, 1, 3, 0):
        at = [pl.ds(16 * n + 4 * k, 4) for k in range(4)]
        psend[n] = (rsum[0, at[0]] + rsum[1, at[1]]) + (rsum[2, at[2]] + rsum[3, at[3]])
    for n, to in zip(PEERS, peers, strict=True):
        send(psend.at[n], pbuf.at[n - 1], p_sem.at[0], p_sem.at[1], to)
    took(pbuf, p_sem.at[1])
    total = psend[0]
    for n in range(3):
        total = total + pbuf[n]
    out_ref[...] = total

    took(cbuf.at[pl.ds(0, 7)], c_sem.at[0])
    for n in range(CHUNKS):
        took(gbuf.at[n], g_send.at[n])
    for n in range(14):
        took(qbuf.at[0, 0, first], q_send.at[n])
    took(ebuf.at[pl.ds(0, 15)], e_sem.at[0])

    @pl.when(m != y // 2)
    def _():
        took(ebuf.at[0], e_sem.at[0])

    took(pbuf, p_sem.at[0])


def shards(*args):
    tokens, gate, up, iproj, oproj, seg, lens, ainv, binv, query = args
    tc = gate.shape[0] // CHUNKS
    dma, vmem = pltpu.SemaphoreType.DMA, pltpu.VMEM
    return pl.pallas_call(
        kernel,
        out_shape=pltpu.VMEM((4, 512), F32),
        in_specs=[pl.BlockSpec(memory_space=pl.ANY)] * 10,
        out_specs=pl.BlockSpec(memory_space=pltpu.VMEM),
        scratch_shapes=[
            vmem(tokens.shape, BF16),
            vmem(gate.shape, BF16),
            vmem(up.shape, BF16),
            vmem(iproj.shape, BF16),
            vmem(oproj.shape, BF16),
            vmem((1, 512), jnp.int32),
            vmem((1, 4), jnp.int32),
            vmem(ainv.shape, F32),
            vmem(binv.shape, F32),
            vmem(query.shape, F32),
            vmem((2, 32, 128), F32),
            vmem((8, 32, 128), F32),
            vmem((CHUNKS, 8, 16, tc), F32),
            vmem((CHUNKS, 7, 16, tc), F32),
            vmem((4, 2, 256, 512), F32),
            vmem((4, 4, 128, 512), BF16),
            vmem((4, 4, 128, 512), BF16),
            vmem((32, 128), F32),
            vmem((16, 16, 128), F32),
            vmem((4, 64, 512), F32),
            vmem((4, 4, 512), F32),
            vmem((3, 4, 512), F32),
            dma((8 + 2 * CHUNKS,)),
            dma((2,)),
            dma((CHUNKS,)),
            dma((CHUNKS,)),
            dma((14,)),
            dma((14,)),
            dma((2,)),
            dma((2,)),
            pltpu.SemaphoreType.REGULAR,
            pltpu.SemaphoreType.REGULAR,
        ],
        compiler_params=pltpu.CompilerParams(
            collective_id=0, has_side_effects=True, vmem_limit_bytes=56 * 2**20
        ),
        cost_estimate=pl.CostEstimate(flops=10**9, bytes_accessed=12 * 10**6, transcendentals=0),
    )(tokens, gate, up, iproj, oproj, seg.reshape(1, 512), lens.reshape(1, 4), ainv, binv, query)


def solution(mesh):
    return jax.shard_map(
        shards,
        mesh=mesh,
        in_specs=(
            P(("dp", "tensor"), None),
            P("dp", "tensor"),
            P("dp", "tensor"),
            P(),
            P("tensor", None),
            P("dp"),
            P("dp"),
            P(),
            P(),
            P("tensor", "dp"),
        ),
        out_specs=P("dp", "tensor"),
        check_vma=False,
    )
```

```python
import jax
import jax.numpy as jnp
from jax import lax
from jax.experimental import pallas as pl
from jax.experimental.pallas import tpu as pltpu
from jax.sharding import PartitionSpec as P

F32, BF16 = jnp.float32, jnp.bfloat16
FAR_FIRST = (4, 3, 5, 2, 6, 1, 7)
PEERS = (2, 1, 3)
CHUNKS = 2
NN = (((1,), (0,)), ((), ()))
NT = (((1,), (1,)), ((), ()))


def mm(a, b, dims):
    return lax.dot_general(a, b, dims, preferred_element_type=F32)


def exact(a, b, dims):
    return lax.dot_general(a, b, dims, precision=lax.Precision.HIGHEST, preferred_element_type=F32)


def split(a):
    hi = a.astype(BF16)
    return hi, (a - hi.astype(F32)).astype(BF16)


def mm3(a, b, dims):
    (ah, al), (bh, bl) = a, b
    return mm(ah, bh, dims) + (mm(ah, bl, dims) + mm(al, bh, dims))


def iota(shape, axis):
    return lax.broadcasted_iota(jnp.int32, shape, axis)


def kernel(
    tokens_hbm, gate_hbm, up_hbm, iproj_hbm, oproj_hbm, seg_hbm, len_hbm, ainv_hbm, binv_hbm, query_hbm,
    out_ref,
    tokens, gate, up, iproj, oproj, seg, lens, ainv, binv, query,
    csend, cbuf, gsend, gbuf, qbuf, qhi, qlo, esend, ebuf, rsum, psend, pbuf,
    load_sem, c_sem, g_send, g_recv, q_send, q_recv, e_sem, p_sem, told, ready,
):
    d, z = lax.axis_index("dp"), lax.axis_index("tensor")
    y, x, c = d // 8, lax.rem(d // 2, 4), lax.rem(d, 2)
    m, jz = z // 4, lax.rem(z, 4)

    def dp(y_to, x_to, c_to):
        return lax.rem(y_to, 4) * 8 + lax.rem(x_to, 4) * 2 + lax.rem(c_to, 2)

    def ring(k):
        return lax.rem(z + k, 8)

    def send(src, dst, s_sem, r_sem, to):
        copy = pltpu.make_async_remote_copy(
            src_ref=src, dst_ref=dst, send_sem=s_sem, recv_sem=r_sem, device_id=to, device_id_type=pl.DeviceIdType.MESH
        )
        copy.start()

    def took(ref, sem):
        pltpu.make_async_copy(ref, ref, sem).wait()

    left, right = (dp(y, x + 3, c), z), (dp(y, x + 1, c), z)
    peers = [(dp(y + k, x, c), z) for k in PEERS]

    tc = gate.shape[0] // CHUNKS
    rows = [pl.ds(n * tc, tc) for n in range(CHUNKS)]
    pairs = [(query_hbm, query), (ainv_hbm, ainv), (binv_hbm, binv), (tokens_hbm, tokens), (iproj_hbm, iproj),
             (oproj_hbm, oproj), (seg_hbm, seg), (len_hbm, lens)]
    for n in range(CHUNKS):
        pairs += [(gate_hbm.at[rows[n]], gate.at[rows[n]]), (up_hbm.at[rows[n]], up.at[rows[n]])]
    loads = [pltpu.make_async_copy(src, dst, load_sem.at[i]) for i, (src, dst) in enumerate(pairs)]
    for load in loads:
        load.start()

    barrier = pltpu.get_barrier_semaphore()
    pair = (dp(y, x, c + 1), z)
    greet = [(dp(y, x, 1), ring(k)) for k in FAR_FIRST]
    greet += [(dp(y + k, x, 1), z) for k in PEERS]
    greet += [(dp(y, x + k, 0), z) for k in (1, 3)] + [pair]

    def signal(sem, to):
        pl.semaphore_signal(sem, inc=1, device_id=to, device_id_type=pl.DeviceIdType.MESH)

    def learn(core, count):
        @pl.when(c == core)
        def _():
            pl.semaphore_wait(barrier, count)
            signal(told, pair)

        @pl.when(c != core)
        def _():
            pl.semaphore_wait(told, 1)

    for to in greet:
        signal(barrier, to)

    first, second = pl.ds(0, 128), pl.ds(128, 128)

    def pass_queries(block, half, i, to):
        ref = qbuf.at[block, c, half]
        send(ref, ref, q_send.at[i], q_recv.at[i], to)

    def took_queries(i):
        took(qbuf.at[0, 0, first], q_recv.at[i])

    def share_queries():
        r, i = iota((256, 256), 0), iota((256, 256), 1)
        shuffle = ((((r >> 4) & 3) << 6) + ((r >> 6) << 4) + (r & 15) == i).astype(BF16)
        loads[0].wait()
        q_hi, q_lo = split(query[...])
        qbuf[x, c] = mm(shuffle, q_hi, NT) + mm(shuffle, q_lo, NT)

        learn(0, 5)
        pass_queries(x, first, 0, left)
        pass_queries(x, second, 1, right)
        pass_queries(x, second, 2, left)
        pass_queries(x, first, 3, right)
        pass_queries(x, first, 6, pair)
        pass_queries(x, second, 7, pair)

    @pl.when(z < 4)
    def _():
        share_queries()

    loads[1].wait()
    r, i = iota((64, 64), 0), iota((64, 64), 1)
    source = (((r >> 2) & 1) << 5) + ((r & 3) << 3) + (r >> 3)
    order = (source == i).astype(F32)
    halves = [(iota((64, 128), 1) == iota((64, 128), 0) + 64 * n).astype(F32) for n in range(2)]
    left_inverse = split(
        jnp.concatenate([exact(exact(order, ainv[n], NN), halves[n], NN) for n in range(2)], axis=0)
    )
    loads[2].wait()
    right_inverse = split(jnp.concatenate([exact(binv[n], halves[n], NN) for n in range(2)], axis=0))

    @pl.when(z >= 4)
    def _():
        share_queries()

    loads[3].wait()
    loads[4].wait()
    codes = mm(tokens[...], iproj[...], NN)
    both = mm3(left_inverse, split(jnp.concatenate([codes, codes], axis=0)), NT)
    low = iota((32, 128), 1) < 64
    for n in range(2):
        csend[n] = jnp.where(low, both[64 * n : 64 * n + 32], both[64 * n + 32 : 64 * n + 64])
    cbuf[z] = csend[m]

    learn(1, 21)
    for k in FAR_FIRST:
        send(csend.at[ring(k) // 4], cbuf.at[z], c_sem.at[0], c_sem.at[1], (d, ring(k)))

    loads[5].wait()
    low = iota((tc, 128), 1) < 64
    for n in range(CHUNKS):
        loads[8 + 2 * n].wait()
        part = mm(gate[rows[n]], oproj[...], NN)
        loads[9 + 2 * n].wait()
        part = jnp.where(low, part, mm(up[rows[n]], oproj[...], NN))
        gsend[n] = mm3(right_inverse, split(part), NT).reshape(8, 16, tc)
        for k in FAR_FIRST:
            send(gsend.at[n, ring(k)], gbuf.at[n, k - 1], g_send.at[n], g_recv.at[n], (d, ring(k)))

    for to in peers:
        signal(ready, to)

    loads[6].wait()
    loads[7].wait()
    weights = [
        jnp.where(seg[...] == g, 1.0 / jnp.broadcast_to(lens[:, g : g + 1], seg.shape).astype(F32), 0.0) for g in range(4)
    ]

    took(cbuf.at[pl.ds(0, 7)], c_sem.at[1])
    low = iota((32, 128), 1) < 64
    upper, lower = [], []
    for n in range(4):
        even, odd = cbuf[2 * n], cbuf[2 * n + 1]
        upper.append(jnp.where(low, even, pltpu.roll(odd, 64, 1)))
        lower.append(jnp.where(low, pltpu.roll(even, 64, 1), odd))
    codes_t = split(jnp.concatenate([jnp.concatenate(upper, axis=1), jnp.concatenate(lower, axis=1)], axis=0))

    after, before, beyond = lax.rem(x + 1, 4), lax.rem(x + 3, 4), lax.rem(x + 2, 4)
    took_queries(0)
    pass_queries(after, first, 4, left)
    pass_queries(after, first, 8, pair)
    took_queries(1)
    pass_queries(before, second, 5, right)
    pass_queries(before, second, 9, pair)

    pl.semaphore_wait(ready, len(peers))

    outer = 0.0
    for n in range(CHUNKS):
        took(gbuf.at[n], g_recv.at[n])
        total = ((gsend[n, z] + gbuf[n, 0]) + (gbuf[n, 1] + gbuf[n, 2])) + ((gbuf[n, 3] + gbuf[n, 4]) + (gbuf[n, 5] + gbuf[n, 6]))
        at = slice(n * tc, (n + 1) * tc)
        hi, lo = split(jnp.concatenate([total * w[:, at] for w in weights], axis=0))
        hi, lo = jnp.concatenate([hi, hi], axis=0), jnp.concatenate([lo, lo], axis=0)
        c_hi, c_lo = codes_t[0][:, at], codes_t[1][:, at]
        outer = outer + mm(jnp.concatenate([c_hi, c_lo, c_hi], axis=1), jnp.concatenate([hi, hi, lo], axis=1), NT)
    turned = [outer] + [pltpu.roll(outer, 16 * k, 1) for k in (1, 2, 3)]
    place = iota((8, 128), 1) >> 4
    for g in range(4):
        piece = turned[(0 - g) % 4][0:8]
        for k in range(1, 8):
            piece = jnp.where(place == k, turned[(k - g) % 4][8 * k : 8 * k + 8], piece)
        esend[pl.ds(g, 8, stride=4), :] = piece

    for zt in (0, 2, 1, 3, 4, 7, 5, 6):
        for n in range(2):
            y_to = 2 * m + n
            src = esend.at[pl.ds(16 * n, 16)]
            dst = ebuf.at[lax.rem(y - y_to + 4, 4) * 4 + jz]
            own = (y == y_to) & (z == zt)

            @pl.when(jnp.logical_not(own))
            def _(src=src, dst=dst, to=(dp(y_to, x, c), zt)):
                send(src, dst, e_sem.at[0], e_sem.at[1], to)

            @pl.when(own)
            def _(src=src, dst=dst):
                pltpu.make_async_copy(src, dst, e_sem.at[1]).start()

    def prepare(block, core, half):
        for n in (0, 1) if half is first else (2, 3):
            hi, lo = split(qbuf[block, core, pl.ds(64 * n, 64)])
            at = pl.ds(pl.multiple_of(core * 64, 64), 64)
            qhi[block, n, at] = hi
            qlo[block, n, at] = lo

    took_queries(2)
    pass_queries(after, second, 10, pair)
    took_queries(3)
    pass_queries(before, first, 11, pair)
    for block, half in ((x, first), (x, second), (after, first), (before, second), (after, second), (before, first)):
        prepare(block, c, half)
    early = ((x, first), (x, second), (after, first), (before, second), (after, second), (before, first))
    for n, (block, half) in enumerate(early):
        took_queries(6 + n)
        prepare(block, 1 - c, half)
    took_queries(4)
    pass_queries(beyond, first, 12, pair)
    took_queries(5)
    pass_queries(beyond, second, 13, pair)
    for n, (core, half) in enumerate(((c, first), (c, second), (1 - c, first), (1 - c, second))):
        if n >= 2:
            took_queries(10 + n)
        prepare(beyond, core, half)

    took(ebuf, e_sem.at[1])
    pieces = ebuf[...].reshape(4, 4, 16, 128)
    e_hi, e_lo = split(jnp.concatenate([pieces[:, n].reshape(64, 128) for n in range(4)], axis=1))
    e_both = jnp.concatenate([e_hi, e_lo], axis=0)
    for n in range(4):
        main = mm(e_both, qhi[n].reshape(512, 512), NN)
        rsum[n] = main[:64] + main[64:] + mm(e_hi, qlo[n].reshape(512, 512), NN)
    for n in (2, 1, 3, 0):
        at = [pl.ds(16 * n + 4 * k, 4) for k in range(4)]
        psend[n] = (rsum[0, at[0]] + rsum[1, at[1]]) + (rsum[2, at[2]] + rsum[3, at[3]])
    for n, to in zip(PEERS, peers, strict=True):
        send(psend.at[n], pbuf.at[n - 1], p_sem.at[0], p_sem.at[1], to)
    took(pbuf, p_sem.at[1])
    total = psend[0]
    for n in range(3):
        total = total + pbuf[n]
    out_ref[...] = total

    took(cbuf.at[pl.ds(0, 7)], c_sem.at[0])
    for n in range(CHUNKS):
        took(gbuf.at[n], g_send.at[n])
    for n in range(14):
        took(qbuf.at[0, 0, first], q_send.at[n])
    took(ebuf.at[pl.ds(0, 15)], e_sem.at[0])

    @pl.when(m != y // 2)
    def _():
        took(ebuf.at[0], e_sem.at[0])

    took(pbuf, p_sem.at[0])


def shards(*args):
    tokens, gate, up, iproj, oproj, seg, lens, ainv, binv, query = args
    tc = gate.shape[0] // CHUNKS
    dma, vmem = pltpu.SemaphoreType.DMA, pltpu.VMEM
    return pl.pallas_call(
        kernel,
        out_shape=pltpu.VMEM((4, 512), F32),
        in_specs=[pl.BlockSpec(memory_space=pl.ANY)] * 10,
        out_specs=pl.BlockSpec(memory_space=pltpu.VMEM),
        scratch_shapes=[
            vmem(tokens.shape, BF16),
            vmem(gate.shape, BF16),
            vmem(up.shape, BF16),
            vmem(iproj.shape, BF16),
            vmem(oproj.shape, BF16),
            vmem((1, 512), jnp.int32),
            vmem((1, 4), jnp.int32),
            vmem(ainv.shape, F32),
            vmem(binv.shape, F32),
            vmem(query.shape, F32),
            vmem((2, 32, 128), F32),
            vmem((8, 32, 128), F32),
            vmem((CHUNKS, 8, 16, tc), F32),
            vmem((CHUNKS, 7, 16, tc), F32),
            vmem((4, 2, 256, 512), F32),
            vmem((4, 4, 128, 512), BF16),
            vmem((4, 4, 128, 512), BF16),
            vmem((32, 128), F32),
            vmem((16, 16, 128), F32),
            vmem((4, 64, 512), F32),
            vmem((4, 4, 512), F32),
            vmem((3, 4, 512), F32),
            dma((8 + 2 * CHUNKS,)),
            dma((2,)),
            dma((CHUNKS,)),
            dma((CHUNKS,)),
            dma((14,)),
            dma((14,)),
            dma((2,)),
            dma((2,)),
            pltpu.SemaphoreType.REGULAR,
            pltpu.SemaphoreType.REGULAR,
        ],
        compiler_params=pltpu.CompilerParams(
            collective_id=0, has_side_effects=True, vmem_limit_bytes=56 * 2**20
        ),
        cost_estimate=pl.CostEstimate(flops=10**9, bytes_accessed=12 * 10**6, transcendentals=0),
    )(tokens, gate, up, iproj, oproj, seg.reshape(1, 512), lens.reshape(1, 4), ainv, binv, query)


def solution(mesh):
    return jax.shard_map(
        shards,
        mesh=mesh,
        in_specs=(
            P(("dp", "tensor"), None),
            P("dp", "tensor"),
            P("dp", "tensor"),
            P(),
            P("tensor", None),
            P("dp"),
            P("dp"),
            P(),
            P(),
            P("tensor", "dp"),
        ),
        out_specs=P("dp", "tensor"),
        check_vma=False,
    )
```
